32 devices in a mesh: grp: 2 (over x), patch: 16 (over z, y, core).
Axes of the slice: x: 2, y: 2, z: 4, core: 2. Of those that a mesh axis runs over, the one named last changes fastest.
Arguments:
- query: bfloat16 [1536, 5120], P(('grp', 'patch')), parts along dimension 0, may hold values from -128 to 128
- fresh_kv: bfloat16 [2, 1536, 5120], P(None, ('grp', 'patch')), parts along dimension 1, may hold values from -6 to 6
- own_stale: bfloat16 [2, 1536, 5120], P(None, ('grp', 'patch')), parts along dimension 1, may hold values from -6 to 6
- caches: bfloat16 [32, 2, 768, 640], P(('grp', 'patch')), parts along dimension 0, may hold values from -6 to 6
- exponents: int32 [2, 1536, 40], P(None, ('grp', 'patch')), parts along dimension 1, may hold values from -2 to 0
Outputs:
- attended: bfloat16 [1536, 5120], P(('grp', 'patch')), parts along dimension 0
- renewed: bfloat16 [2, 1536, 5120], P(None, ('grp', 'patch')), parts along dimension 1
The draws below stay inside these ranges and needn't reach their ends.
There are 2 independent parts, one for each index of `grp`. The reference program is written for one: setup_inputs(seed, part) draws one part's arguments, and reference() takes and returns one part's arrays. A program takes and returns all parts, laid end to end along the dimension named above; each array names one. Nothing has to cross between parts.
All inputs are finite; a program needn't handle non-finite values.
Results may differ from the reference program's by a relative error of at most 0.0091.
Values may be sent and summed in bfloat16 or wider, within the bound.
A program may use at most 128 MiB of HBM per device.

```python
import jax
import jax.numpy as jnp
from jax import lax

D = 5120
HEADS = 40
HEAD = 128
HG = 8
TOK_DEV = 48
TOKENS = 768
SL = 2
SUB = 24
GCOLS = 640
N_PATCH = 16


def base_keys(key):
    return jnp.clip(jax.random.normal(key, (TOKENS, D), jnp.float32), -6.0, 6.0)


def draw_query(key, part):
    key = jax.random.fold_in(key, 11)
    query_all = jnp.clip(jax.random.normal(key, (TOKENS, D), jnp.float32), -4.0, 4.0)
    return jnp.clip(query_all, -128.0, 128.0).astype(jnp.bfloat16)


def draw_fresh_kv(key, part):
    keys_all = base_keys(key)
    key = jax.random.fold_in(key, 7)
    values_all = jnp.clip(jax.random.normal(key, (TOKENS, D), jnp.float32), -6.0, 6.0)
    return jnp.stack([keys_all, values_all]).astype(jnp.bfloat16)


def set_ends(array, key, least, largest):
    longest = array.shape.index(max(array.shape))
    spots = []
    for shift in (0, 1):
        where = [jax.random.randint(jax.random.fold_in(key, axis), (), 0, length) for axis, length in enumerate(array.shape)]
        where[longest] = (where[longest] + shift) % array.shape[longest]
        spots.append(tuple(where))
    return array.at[spots[0]].set(least).at[spots[1]].set(largest)


def levels(key, dims, cuts, low, top_value):
    gain = 1.0
    for axis_at, blocks in cuts:
        draws = jax.random.uniform(jax.random.fold_in(jax.random.fold_in(key, 6), axis_at), (blocks,), jnp.float32, low / len(cuts), top_value / len(cuts))
        gain = gain * jnp.repeat(jnp.exp(draws), dims[axis_at] // blocks).reshape((-1,) + (1,) * (len(dims) - 1 - axis_at))
    return gain


def normal_values(stream_key, dims, spread, limit, shards=(), held_as=jnp.bfloat16):
    gain = levels(stream_key, dims, shards, -0.22, 0.18) if shards else 1.0
    array = jax.random.normal(stream_key, dims, jnp.float32) * spread * gain
    return jnp.minimum(jnp.maximum(array, -limit), limit).astype(held_as)


def setup_inputs(seed: int = 0, part: int = 0) -> dict:
    arg_keys = jax.random.split(jax.random.key(seed), 6)
    part_keys = jax.random.split(jax.random.fold_in(arg_keys[5], part), 6)
    query = draw_query(jax.random.fold_in(jax.random.fold_in(arg_keys[5], part), 71), part)
    fresh_kv = draw_fresh_kv(jax.random.fold_in(jax.random.fold_in(arg_keys[5], part), 71), part)
    own_stale = normal_values(part_keys[2], (2, TOKENS, D), 1.0, 6.0, ((1, 16),))
    caches = normal_values(part_keys[3], (N_PATCH, 2, TOKENS, GCOLS), 1.0, 6.0, ((0, 16),))
    exponents = set_ends(jax.random.randint(part_keys[4], (2, TOKENS, HEADS), -2, 1), jax.random.fold_in(part_keys[4], 1), -2, 0).astype(jnp.int32)
    return {"query": query, "fresh_kv": fresh_kv, "own_stale": own_stale, "caches": caches, "exponents": exponents}


LIMIT = 8.0


def device_attention(position, query, fresh_kv, caches, decoded):
    zero = jnp.zeros((), jnp.int32)
    head_group = (position // SL).astype(jnp.int32)
    slab_slot = (position % SL).astype(jnp.int32)
    group_heads = HEADS // HG
    slab_count = TOKENS // TOK_DEV
    column_start = (head_group * GCOLS).astype(jnp.int32)
    shared = lax.dynamic_slice(decoded, (zero, zero, column_start), (2, TOKENS, GCOLS))
    mine = lax.dynamic_index_in_dim(caches, position, 0, keepdims=False)
    stored = (mine.astype(jnp.float32) + shared.astype(jnp.float32)).astype(jnp.bfloat16)
    row_start = (position * TOK_DEV).astype(jnp.int32)
    local_rows = lax.dynamic_slice(fresh_kv, (zero, row_start, column_start), (2, TOK_DEV, GCOLS))
    stored = lax.dynamic_update_slice(stored, local_rows, (zero, row_start, zero))
    blocks = query.reshape(slab_count, TOK_DEV, D)
    sub_start = (slab_slot * SUB).astype(jnp.int32)
    chosen = lax.dynamic_slice(blocks, (zero, sub_start, column_start), (slab_count, SUB, GCOLS))
    chosen = chosen.reshape(slab_count * SUB, group_heads, HEAD).astype(jnp.float32)
    key_rows = stored[0].reshape(TOKENS, group_heads, HEAD).astype(jnp.float32)
    value_rows = stored[1].reshape(TOKENS, group_heads, HEAD).astype(jnp.float32)
    scores = jnp.einsum('rhd,khd->hrk', chosen, key_rows) * (HEAD ** -0.5)
    peak = jnp.max(scores, axis=-1, keepdims=True)
    raised = jnp.exp(scores - peak)
    weights = (raised / jnp.sum(raised, axis=-1, keepdims=True)).astype(jnp.bfloat16)
    mixed = jnp.einsum('hrk,khd->rhd', weights.astype(jnp.float32), value_rows)
    return mixed.astype(jnp.bfloat16).reshape(slab_count, SUB, GCOLS)


def reference(query, fresh_kv, own_stale, caches, exponents):
    residual = (fresh_kv.astype(jnp.float32) - own_stale.astype(jnp.float32)).reshape(2, TOKENS, HEADS, HEAD)
    exponent_f = exponents.astype(jnp.float32)[..., None]
    coded = jnp.clip(residual * jnp.exp2(-exponent_f), -LIMIT, LIMIT).astype(jnp.bfloat16)
    decoded = (coded.astype(jnp.float32) * jnp.exp2(exponent_f)).astype(jnp.bfloat16).reshape(2, TOKENS, D)
    renewed = (own_stale.astype(jnp.float32) + decoded.astype(jnp.float32)).astype(jnp.bfloat16)
    slab_count = TOKENS // TOK_DEV
    results = lax.map(lambda position: device_attention(position, query, fresh_kv, caches, decoded), jnp.arange(slab_count, dtype=jnp.int32))
    attended = results.reshape(HG, SL, slab_count, SUB, GCOLS).transpose(2, 1, 3, 0, 4).reshape(TOKENS, D)
    return attended, renewed
```

```python
import functools
import math

import jax
import jax.numpy as jnp
from jax import lax
from jax.experimental import pallas as pl
from jax.experimental.pallas import tpu as pltpu
from jax.sharding import PartitionSpec as P

HG = 8
LIMIT = 8.0
MESH = pl.DeviceIdType.MESH
ORDER = (4, 6, 5, 7, 2, 3, 1, 0)


def round_up(value, step):
    return -(-value // step) * step


def partner_group(group, k):
    total = 0
    for b in range(HG.bit_length() - 1):
        bit = lax.rem(lax.div(group, 1 << b), 2)
        total = total + (1 << b) * ((1 - bit) if (k >> b) & 1 else bit)
    return total


def loop(low, high, body):
    if high - low <= 2:
        for i in range(low, high):
            body(i)
    else:

        def step(i, carry):
            body(i)
            return carry

        lax.fori_loop(low, high, step, 0)


def kernel(
    sizes, query, fresh, stale, caches, exps, attended, renewed,
    q_v, f_v, s_v, c_v, e_v, lim, dec, att, ren, keys, values,
    qsend0, qsend1, qsend2, qgot0, qgot1, qgot2, osend0, osend1, osend2, ogot0, ogot1, ogot2,
    arrived, in_sem, out_sem, kv_send, kv_recv, fw_send, q_send, q_recv, o_send, o_recv,
):
    n, spread, rows, sub, unit, head, group_heads, stages = sizes
    cols = group_heads * head
    qsend, qgot = (qsend0, qsend1, qsend2), (qgot0, qgot1, qgot2)
    osend, ogot = (osend0, osend1, osend2), (ogot0, ogot1, ogot2)
    me = lax.axis_index("patch")
    group, member = lax.div(me, spread), lax.rem(me, spread)
    my_rows = pl.ds(pl.multiple_of(me * rows, 16), rows)

    loads = [
        pltpu.make_async_copy(a, b, in_sem.at[i])
        for i, (a, b) in enumerate(
            ((exps, e_v), (fresh, f_v), (stale, s_v), (query, q_v), (caches, c_v))
        )
    ]
    for load in loads:
        load.start()

    barrier = pltpu.get_barrier_semaphore()

    def greet(k):
        pl.semaphore_signal(
            barrier, inc=1, device_id={"patch": lax.rem(me + k, n)}, device_id_type=MESH
        )

    loop(1, n, greet)

    def remote(src, dst, send_sem, recv_sem, device):
        return pltpu.make_async_remote_copy(
            src_ref=src, dst_ref=dst, send_sem=send_sem, recv_sem=recv_sem,
            device_id={"patch": device}, device_id_type=MESH,
        )

    def slab_rows(p):
        return pl.ds(pl.multiple_of(p * rows, 16), rows)

    def landed(s, p):
        first, count = stages[s]
        return arrived.at[pl.ds(first, count), :, slab_rows(p), :]

    def kv_copy(s, go):
        first, count = stages[s]
        return remote(
            dec.at[go, pl.ds(first, count)], landed(s, me),
            kv_send.at[s, go], kv_recv.at[s, me], go * spread + member,
        )

    def forward_copy(s, p, t):
        return remote(
            landed(s, p), landed(s, p),
            fw_send.at[s, lax.div(p, spread), t], kv_recv.at[s, p], group * spread + t,
        )

    def q_copy(s, d):
        return remote(qsend[s].at[d], qgot[s].at[me], q_send.at[s, d], q_recv.at[s, me], d)

    def o_copy(s, p):
        return remote(osend[s].at[p], ogot[s].at[me], o_send.at[s, p], o_recv.at[s, me], p)

    def spread_rows(x):
        if unit == sub:
            return x
        out = lax.broadcasted_iota(jnp.int32, (spread * unit, rows), 0)
        src = lax.broadcasted_iota(jnp.int32, (spread * unit, rows), 1)
        pick = (out // unit * sub + out % unit == src) & (out % unit < sub)
        return jnp.dot(
            pick.astype(jnp.bfloat16), x.astype(jnp.bfloat16), preferred_element_type=jnp.float32
        )

    def join_rows(x):
        if unit == sub:
            return x
        out = lax.broadcasted_iota(jnp.int32, (rows, spread * unit), 0)
        src = lax.broadcasted_iota(jnp.int32, (rows, spread * unit), 1)
        pick = out // sub * unit + out % sub == src
        return jnp.dot(
            pick.astype(jnp.bfloat16), x.astype(jnp.bfloat16), preferred_element_type=jnp.float32
        )

    loads[0].wait()
    head_count = e_v.shape[2]
    lim[...] = (LIMIT * jnp.exp2(e_v[...].astype(jnp.float32))).reshape(2 * rows, head_count).astype(
        jnp.bfloat16
    )
    for load in loads[1:4]:
        load.wait()

    def prepare(s, go):
        first, count = stages[s]
        width = count * head
        start = pl.multiple_of(go * cols + first * head, 128)
        window = pl.ds(start, width)
        which = lax.broadcasted_iota(jnp.int32, (head_count, width), 0)
        column = lax.broadcasted_iota(jnp.int32, (head_count, width), 1)
        one_hot = (which == go * group_heads + first + column // head).astype(jnp.bfloat16)
        limit = jnp.dot(lim[...], one_hot, preferred_element_type=jnp.float32)
        limit = limit.reshape(2, rows, width)
        old = s_v[:, :, window].astype(jnp.float32)
        residual = f_v[:, :, window].astype(jnp.float32) - old
        decoded = jnp.clip(residual, -limit, limit).astype(jnp.bfloat16)
        for j in range(count):
            dec[go, first + j] = decoded[:, :, j * head : (j + 1) * head]
        ren[:, :, window] = (old + decoded.astype(jnp.float32)).astype(jnp.bfloat16)
        block = spread_rows(q_v[:, window].astype(jnp.float32))
        for t in range(spread):
            parts = [
                block[t * unit : (t + 1) * unit, j * head : (j + 1) * head] for j in range(count)
            ]
            spare = qsend[s].shape[1] - count * unit
            if spare:
                parts.append(jnp.zeros((spare, head), jnp.float32))
            qsend[s][go * spread + t] = jnp.concatenate(parts, axis=0).astype(jnp.bfloat16)

    for s in range(len(stages)):
        first, count = stages[s]
        for k in ORDER:
            go = partner_group(group, k)
            prepare(s, go)
            if s == 0 and k == ORDER[0]:
                pl.semaphore_wait(barrier, n - 1)
            if k:
                kv_copy(s, go).start()
                loop(0, spread, lambda t: q_copy(s, go * spread + t).start())
            else:
                arrived[pl.ds(first, count), :, my_rows, :] = dec[group, pl.ds(first, count)]
                qgot[s][me] = qsend[s][me]

                def to_sibling(t):
                    @pl.when(t != member)
                    def _():
                        forward_copy(s, me, t).start()
                        q_copy(s, group * spread + t).start()

                loop(0, spread, to_sibling)

    write_renewed = pltpu.make_async_copy(ren, renewed, out_sem.at[0])
    write_renewed.start()
    loads[4].wait()

    def unpack(s):
        first, count = stages[s]

        def one_group(g):
            def arrive(t):
                @pl.when(g * spread + t != me)
                def _():
                    p = g * spread + t
                    remote(
                        osend[s].at[p], ogot[s].at[p], o_send.at[s, p], o_recv.at[s, p], p
                    ).wait_recv()

            loop(0, spread, arrive)
            got = ogot[s][pl.ds(g * spread, spread)].astype(jnp.float32)
            for j in range(count):
                piece = got[:, j * unit : (j + 1) * unit, :].reshape(spread * unit, head)
                start = pl.multiple_of(g * cols + (first + j) * head, 128)
                att[:, pl.ds(start, head)] = join_rows(piece).astype(jnp.bfloat16)

        loop(0, HG, one_group)

    scale = head ** (-0.5) * math.log2(math.e)
    chunk = 8
    for s in range(len(stages)):
        first, count = stages[s]
        for k in ORDER[:-1]:
            p = partner_group(group, k) * spread + member
            forward_copy(s, p, 0).wait_recv()

            def pass_on(t):
                @pl.when(t != member)
                def _():
                    forward_copy(s, p, t).start()

            loop(0, spread, pass_on)

        def arrive_q(k):
            p = lax.rem(me + k, n)
            remote(qsend[s].at[p], qgot[s].at[p], q_send.at[s, p], q_recv.at[s, p], p).wait_recv()

        loop(1, n, arrive_q)

        def arrive_kv(t):
            @pl.when(t != member)
            def _():
                def one(g):
                    forward_copy(s, g * spread + t, 0).wait_recv()

                loop(0, HG, one)

        loop(0, spread, arrive_kv)

        for j in range(count):
            columns = pl.ds((first + j) * head, head)
            mine = pl.ds(pl.multiple_of(group * cols + (first + j) * head, 128), head)
            for which, store in ((0, keys), (1, values)):
                store[j] = (
                    c_v[0, which, :, columns].astype(jnp.float32)
                    + arrived[first + j, which].astype(jnp.float32)
                ).astype(jnp.bfloat16)
                store[j, my_rows, :] = f_v[which, :, mine]

        for c0 in range(0, n, chunk):
            block = qgot[s][c0 : c0 + chunk].astype(jnp.float32)
            outs = []
            for j in range(count):
                q = block[:, j * unit : (j + 1) * unit, :].reshape(chunk * unit, head)
                scores = lax.dot_general(
                    q.astype(jnp.bfloat16), keys[j], (((1,), (1,)), ((), ())),
                    preferred_element_type=jnp.float32,
                )
                peak = jnp.max(scores, axis=-1, keepdims=True)
                raised = jnp.exp2((scores - peak) * scale)
                total = jnp.sum(raised, axis=-1, keepdims=True)
                mixed = jnp.dot(
                    raised.astype(jnp.bfloat16), values[j], preferred_element_type=jnp.float32
                )
                outs.append((mixed / total).reshape(chunk, unit, head))
            spare = osend[s].shape[1] - count * unit
            if spare:
                outs.append(jnp.zeros((chunk, spare, head), jnp.float32))
            osend[s][c0 : c0 + chunk] = jnp.concatenate(outs, axis=1).astype(jnp.bfloat16)

            def give_back(i):
                p = c0 + i

                @pl.when(p != me)
                def _():
                    o_copy(s, p).start()

                @pl.when(p == me)
                def _():
                    ogot[s][me] = osend[s][me]

            loop(0, chunk, give_back)

    for s in range(len(stages)):
        unpack(s)
    write_attended = pltpu.make_async_copy(att, attended, out_sem.at[1])
    write_attended.start()

    for s in range(len(stages)):

        def left(k):
            p = lax.rem(me + k, n)
            q_copy(s, p).wait_send()
            o_copy(s, p).wait_send()

        loop(1, n, left)
        for k in ORDER[:-1]:
            kv_copy(s, partner_group(group, k)).wait_send()

        def left_sibling(t):
            @pl.when(t != member)
            def _():
                def one(g):
                    forward_copy(s, g * spread + member, t).wait_send()

                loop(0, HG, one)

        loop(0, spread, left_sibling)
    write_renewed.wait()
    write_attended.wait()


def local(query, fresh_kv, own_stale, caches, exponents):
    rows, width = query.shape
    n = lax.axis_size("patch")
    spread = n // HG
    sub = rows // spread
    head = width // exponents.shape[2]
    group_heads = exponents.shape[2] // HG
    cols = width // HG
    unit = round_up(sub, 8)
    cuts = (0, 2, 4, group_heads)
    stages = tuple((a, b - a) for a, b in zip(cuts[:-1], cuts[1:]))
    tokens = caches.shape[2]
    most = max(count for _, count in stages)
    bf16 = jnp.bfloat16
    packs = [(n, round_up(count * unit, 16), head) for _, count in stages]
    dma = pltpu.SemaphoreType.DMA
    ns = len(stages)
    scratch = (
        [
            pltpu.VMEM(query.shape, bf16),
            pltpu.VMEM(fresh_kv.shape, bf16),
            pltpu.VMEM(own_stale.shape, bf16),
            pltpu.VMEM(caches.shape, bf16),
            pltpu.VMEM(exponents.shape, jnp.int32),
            pltpu.VMEM((2 * rows, exponents.shape[2]), bf16),
            pltpu.VMEM((HG, group_heads, 2, rows, head), bf16),
            pltpu.VMEM(query.shape, bf16),
            pltpu.VMEM(fresh_kv.shape, bf16),
            pltpu.VMEM((most, tokens, head), bf16),
            pltpu.VMEM((most, tokens, head), bf16),
        ]
        + [pltpu.VMEM(pack, bf16) for _ in range(4) for pack in packs]
        + [
            pltpu.VMEM((group_heads, 2, tokens, head), bf16),
            dma((5,)),
            dma((2,)),
            dma((ns, HG)),
            dma((ns, n)),
            dma((ns, HG, spread)),
            dma((ns, n)),
            dma((ns, n)),
            dma((ns, n)),
            dma((ns, n)),
        ]
    )
    sizes = (n, spread, rows, sub, unit, head, group_heads, stages)
    anywhere = pl.BlockSpec(memory_space=pl.ANY)
    return pl.pallas_call(
        functools.partial(kernel, sizes),
        out_shape=(
            jax.ShapeDtypeStruct(query.shape, bf16),
            jax.ShapeDtypeStruct(fresh_kv.shape, bf16),
        ),
        in_specs=[anywhere] * 5,
        out_specs=(anywhere, anywhere),
        scratch_shapes=scratch,
        compiler_params=pltpu.CompilerParams(
            collective_id=0, has_side_effects=True, vmem_limit_bytes=48 * 1024 * 1024
        ),
    )(query, fresh_kv, own_stale, caches, exponents)


def solution(mesh):
    return jax.shard_map(
        local,
        mesh=mesh,
        in_specs=(
            P(("grp", "patch"), None),
            P(None, ("grp", "patch"), None),
            P(None, ("grp", "patch"), None),
            P(("grp", "patch"), None, None, None),
            P(None, ("grp", "patch"), None),
        ),
        out_specs=(P(("grp", "patch"), None), P(None, ("grp", "patch"), None)),
        check_vma=False,
    )
```

```python
import functools
import math

import jax
import jax.numpy as jnp
from jax import lax
from jax.experimental import pallas as pl
from jax.experimental.pallas import tpu as pltpu
from jax.sharding import PartitionSpec as P

HG = 8
LIMIT = 8.0
MESH = pl.DeviceIdType.MESH
ORDER = (4, 6, 5, 7, 2, 3, 1, 0)


def round_up(value, step):
    return -(-value // step) * step


def partner_group(group, k):
    total = 0
    for b in range(HG.bit_length() - 1):
        bit = lax.rem(lax.div(group, 1 << b), 2)
        total = total + (1 << b) * ((1 - bit) if (k >> b) & 1 else bit)
    return total


def loop(low, high, body):
    if high - low <= 2:
        for i in range(low, high):
            body(i)
    else:

        def step(i, carry):
            body(i)
            return carry

        lax.fori_loop(low, high, step, 0)


def kernel(
    sizes, query, fresh, stale, caches, exps, attended, renewed,
    q_v, f_v, s_v, c_v, e_v, lim, dec, att, ren, keys, values,
    qsend0, qsend1, qsend2, qgot0, qgot1, qgot2, osend0, osend1, osend2, ogot0, ogot1, ogot2,
    arrived, in_sem, out_sem, kv_send, kv_recv, fw_send, q_send, q_recv, o_send, o_recv,
):
    n, spread, rows, sub, unit, head, group_heads, stages = sizes
    cols = group_heads * head
    qsend, qgot = (qsend0, qsend1, qsend2), (qgot0, qgot1, qgot2)
    osend, ogot = (osend0, osend1, osend2), (ogot0, ogot1, ogot2)
    me = lax.axis_index("patch")
    group, member = lax.div(me, spread), lax.rem(me, spread)
    my_rows = pl.ds(pl.multiple_of(me * rows, 16), rows)

    loads = [
        pltpu.make_async_copy(a, b, in_sem.at[i])
        for i, (a, b) in enumerate(
            ((exps, e_v), (fresh, f_v), (stale, s_v), (query, q_v), (caches, c_v))
        )
    ]
    for load in loads[:4]:
        load.start()

    barrier = pltpu.get_barrier_semaphore()

    def greet(k):
        pl.semaphore_signal(
            barrier, inc=1, device_id={"patch": lax.rem(me + k, n)}, device_id_type=MESH
        )

    loop(1, n, greet)

    def remote(src, dst, send_sem, recv_sem, device):
        return pltpu.make_async_remote_copy(
            src_ref=src, dst_ref=dst, send_sem=send_sem, recv_sem=recv_sem,
            device_id={"patch": device}, device_id_type=MESH,
        )

    def slab_rows(p):
        return pl.ds(pl.multiple_of(p * rows, 16), rows)

    def landed(s, p):
        first, count = stages[s]
        return arrived.at[pl.ds(first, count), :, slab_rows(p), :]

    def kv_copy(s, go):
        first, count = stages[s]
        return remote(
            dec.at[go, pl.ds(first, count)], landed(s, me),
            kv_send.at[s, go], kv_recv.at[s, me], go * spread + member,
        )

    def forward_copy(s, p, t):
        return remote(
            landed(s, p), landed(s, p),
            fw_send.at[s, lax.div(p, spread), t], kv_recv.at[s, p], group * spread + t,
        )

    def q_copy(s, d):
        return remote(qsend[s].at[d], qgot[s].at[me], q_send.at[s, d], q_recv.at[s, me], d)

    def o_copy(s, p):
        return remote(osend[s].at[p], ogot[s].at[me], o_send.at[s, p], o_recv.at[s, me], p)

    def spread_rows(x):
        if unit == sub:
            return x
        out = lax.broadcasted_iota(jnp.int32, (spread * unit, rows), 0)
        src = lax.broadcasted_iota(jnp.int32, (spread * unit, rows), 1)
        pick = (out // unit * sub + out % unit == src) & (out % unit < sub)
        return jnp.dot(
            pick.astype(jnp.bfloat16), x.astype(jnp.bfloat16), preferred_element_type=jnp.float32
        )

    def join_rows(x):
        if unit == sub:
            return x
        out = lax.broadcasted_iota(jnp.int32, (rows, spread * unit), 0)
        src = lax.broadcasted_iota(jnp.int32, (rows, spread * unit), 1)
        pick = out // sub * unit + out % sub == src
        return jnp.dot(
            pick.astype(jnp.bfloat16), x.astype(jnp.bfloat16), preferred_element_type=jnp.float32
        )

    loads[0].wait()
    head_count = e_v.shape[1]
    turn = lax.broadcasted_iota(jnp.int32, (head_count, head_count), 0)
    turn = (turn == lax.broadcasted_iota(jnp.int32, (head_count, head_count), 1)).astype(jnp.bfloat16)
    for which in (0, 1):
        power = (LIMIT * jnp.exp2(e_v[which].astype(jnp.float32))).astype(jnp.bfloat16)
        lim[which * rows : (which + 1) * rows] = lax.dot_general(
            power, turn, (((0,), (0,)), ((), ())), preferred_element_type=jnp.float32
        ).astype(jnp.bfloat16)
    for load in loads[1:4]:
        load.wait()

    def prepare(s, go):
        first, count = stages[s]
        width = count * head
        start = pl.multiple_of(go * cols + first * head, 128)
        window = pl.ds(start, width)
        which = lax.broadcasted_iota(jnp.int32, (head_count, width), 0)
        column = lax.broadcasted_iota(jnp.int32, (head_count, width), 1)
        one_hot = (which == go * group_heads + first + column // head).astype(jnp.bfloat16)
        limit = jnp.dot(lim[...], one_hot, preferred_element_type=jnp.float32)
        limit = limit.reshape(2, rows, width)
        old = s_v[:, :, window].astype(jnp.float32)
        residual = f_v[:, :, window].astype(jnp.float32) - old
        decoded = jnp.clip(residual, -limit, limit).astype(jnp.bfloat16)
        for j in range(count):
            dec[go, first + j] = decoded[:, :, j * head : (j + 1) * head]
        ren[:, :, window] = (old + decoded.astype(jnp.float32)).astype(jnp.bfloat16)
        block = spread_rows(q_v[:, window].astype(jnp.float32))
        for t in range(spread):
            parts = [
                block[t * unit : (t + 1) * unit, j * head : (j + 1) * head] for j in range(count)
            ]
            spare = qsend[s].shape[1] - count * unit
            if spare:
                parts.append(jnp.zeros((spare, head), jnp.float32))
            qsend[s][go * spread + t] = jnp.concatenate(parts, axis=0).astype(jnp.bfloat16)

    for k in ORDER:
        prepare(0, partner_group(group, k))
    pl.semaphore_wait(barrier, n - 1)
    loads[4].start()

    for s in range(len(stages)):
        first, count = stages[s]
        for k in ORDER:
            go = partner_group(group, k)
            if s:
                prepare(s, go)
            if k:
                kv_copy(s, go).start()
                loop(0, spread, lambda t: q_copy(s, go * spread + t).start())
            else:
                arrived[pl.ds(first, count), :, my_rows, :] = dec[group, pl.ds(first, count)]
                qgot[s][me] = qsend[s][me]

                def to_sibling(t):
                    @pl.when(t != member)
                    def _():
                        forward_copy(s, me, t).start()
                        q_copy(s, group * spread + t).start()

                loop(0, spread, to_sibling)

    write_renewed = pltpu.make_async_copy(ren, renewed, in_sem.at[5])
    write_renewed.start()
    loads[4].wait()

    def write_group(s, g):
        first, count = stages[s]
        window = pl.ds(pl.multiple_of(g * cols + first * head, 128), count * head)
        return pltpu.make_async_copy(att.at[:, window], attended.at[:, window], out_sem.at[s, g])

    def unpack(s):
        first, count = stages[s]

        def one_group(g):
            def arrive(t):
                @pl.when(g * spread + t != me)
                def _():
                    p = g * spread + t
                    remote(
                        osend[s].at[p], ogot[s].at[p], o_send.at[s, p], o_recv.at[s, p], p
                    ).wait_recv()

            loop(0, spread, arrive)
            got = ogot[s][pl.ds(g * spread, spread)].astype(jnp.float32)
            for j in range(count):
                piece = got[:, j * unit : (j + 1) * unit, :].reshape(spread * unit, head)
                start = pl.multiple_of(g * cols + (first + j) * head, 128)
                att[:, pl.ds(start, head)] = join_rows(piece).astype(jnp.bfloat16)
            write_group(s, g).start()

        loop(0, HG, one_group)

    scale = head ** (-0.5) * math.log2(math.e)
    chunk = 8
    for s in range(len(stages)):
        first, count = stages[s]
        for k in ORDER[:-1]:
            p = partner_group(group, k) * spread + member
            forward_copy(s, p, 0).wait_recv()

            def pass_on(t):
                @pl.when(t != member)
                def _():
                    forward_copy(s, p, t).start()

            loop(0, spread, pass_on)

        def arrive_q(k):
            p = lax.rem(me + k, n)
            remote(qsend[s].at[p], qgot[s].at[p], q_send.at[s, p], q_recv.at[s, p], p).wait_recv()

        loop(1, n, arrive_q)

        def arrive_kv(t):
            @pl.when(t != member)
            def _():
                def one(g):
                    forward_copy(s, g * spread + t, 0).wait_recv()

                loop(0, HG, one)

        loop(0, spread, arrive_kv)

        for j in range(count):
            columns = pl.ds((first + j) * head, head)
            mine = pl.ds(pl.multiple_of(group * cols + (first + j) * head, 128), head)
            for which, store in ((0, keys), (1, values)):
                store[j] = (
                    c_v[0, which, :, columns].astype(jnp.float32)
                    + arrived[first + j, which].astype(jnp.float32)
                ).astype(jnp.bfloat16)
                store[j, my_rows, :] = f_v[which, :, mine]

        for c0 in range(0, n, chunk):
            block = qgot[s][c0 : c0 + chunk].astype(jnp.float32)
            outs = []
            for j in range(count):
                q = block[:, j * unit : (j + 1) * unit, :].reshape(chunk * unit, head)
                scores = lax.dot_general(
                    q.astype(jnp.bfloat16), keys[j], (((1,), (1,)), ((), ())),
                    preferred_element_type=jnp.float32,
                )
                peak = jnp.max(scores, axis=-1, keepdims=True)
                raised = jnp.exp2((scores - peak) * scale)
                total = jnp.sum(raised, axis=-1, keepdims=True)
                mixed = jnp.dot(
                    raised.astype(jnp.bfloat16), values[j], preferred_element_type=jnp.float32
                )
                outs.append((mixed / total).reshape(chunk, unit, head))
            spare = osend[s].shape[1] - count * unit
            if spare:
                outs.append(jnp.zeros((chunk, spare, head), jnp.float32))
            osend[s][c0 : c0 + chunk] = jnp.concatenate(outs, axis=1).astype(jnp.bfloat16)

            def give_back(i):
                p = c0 + i

                @pl.when(p != me)
                def _():
                    o_copy(s, p).start()

                @pl.when(p == me)
                def _():
                    ogot[s][me] = osend[s][me]

            loop(0, chunk, give_back)

    for s in range(len(stages)):
        unpack(s)

    for s in range(len(stages)):

        def left(k):
            p = lax.rem(me + k, n)
            q_copy(s, p).wait_send()
            o_copy(s, p).wait_send()

        loop(1, n, left)
        for k in ORDER[:-1]:
            kv_copy(s, partner_group(group, k)).wait_send()

        def left_sibling(t):
            @pl.when(t != member)
            def _():
                def one(g):
                    forward_copy(s, g * spread + member, t).wait_send()

                loop(0, HG, one)

        loop(0, spread, left_sibling)
    write_renewed.wait()
    for s in range(len(stages)):
        loop(0, HG, lambda g: write_group(s, g).wait())


def local(query, fresh_kv, own_stale, caches, exponents):
    rows, width = query.shape
    n = lax.axis_size("patch")
    spread = n // HG
    sub = rows // spread
    head = width // exponents.shape[2]
    group_heads = exponents.shape[2] // HG
    cols = width // HG
    unit = round_up(sub, 8)
    cuts = (0, 2, 4, group_heads)
    stages = tuple((a, b - a) for a, b in zip(cuts[:-1], cuts[1:]))
    tokens = caches.shape[2]
    most = max(count for _, count in stages)
    bf16 = jnp.bfloat16
    packs = [(n, round_up(count * unit, 16), head) for _, count in stages]
    dma = pltpu.SemaphoreType.DMA
    ns = len(stages)
    scratch = (
        [
            pltpu.VMEM(query.shape, bf16),
            pltpu.VMEM(fresh_kv.shape, bf16),
            pltpu.VMEM(own_stale.shape, bf16),
            pltpu.VMEM(caches.shape, bf16),
            pltpu.VMEM((2, exponents.shape[2], rows), jnp.int32),
            pltpu.VMEM((2 * rows, exponents.shape[2]), bf16),
            pltpu.VMEM((HG, group_heads, 2, rows, head), bf16),
            pltpu.VMEM(query.shape, bf16),
            pltpu.VMEM(fresh_kv.shape, bf16),
            pltpu.VMEM((most, tokens, head), bf16),
            pltpu.VMEM((most, tokens, head), bf16),
        ]
        + [pltpu.VMEM(pack, bf16) for _ in range(4) for pack in packs]
        + [
            pltpu.VMEM((group_heads, 2, tokens, head), bf16),
            dma((6,)),
            dma((ns, HG)),
            dma((ns, HG)),
            dma((ns, n)),
            dma((ns, HG, spread)),
            dma((ns, n)),
            dma((ns, n)),
            dma((ns, n)),
            dma((ns, n)),
        ]
    )
    sizes = (n, spread, rows, sub, unit, head, group_heads, stages)
    anywhere = pl.BlockSpec(memory_space=pl.ANY)
    return pl.pallas_call(
        functools.partial(kernel, sizes),
        out_shape=(
            pltpu.VMEM(query.shape, bf16),
            pltpu.VMEM(fresh_kv.shape, bf16),
        ),
        in_specs=[pl.BlockSpec(memory_space=pltpu.HBM)] * 5,
        out_specs=(anywhere, anywhere),
        scratch_shapes=scratch,
        compiler_params=pltpu.CompilerParams(
            collective_id=0, has_side_effects=True, vmem_limit_bytes=60 * 1024 * 1024
        ),
    )(query, fresh_kv, own_stale, caches, exponents.transpose(0, 2, 1))


def solution(mesh):
    return jax.shard_map(
        local,
        mesh=mesh,
        in_specs=(
            P(("grp", "patch"), None),
            P(None, ("grp", "patch"), None),
            P(None, ("grp", "patch"), None),
            P(("grp", "patch"), None, None, None),
            P(None, ("grp", "patch"), None),
        ),
        out_specs=(P(("grp", "patch"), None), P(None, ("grp", "patch"), None)),
        check_vma=False,
    )
```

```python
import functools
import math

import jax
import jax.numpy as jnp
from jax import lax
from jax.experimental import pallas as pl
from jax.experimental.pallas import tpu as pltpu
from jax.sharding import PartitionSpec as P

HG = 8
LIMIT = 8.0
MESH = pl.DeviceIdType.MESH
ORDER = (4, 6, 5, 7, 2, 3, 1, 0)


def round_up(value, step):
    return -(-value // step) * step


def partner_group(group, k):
    total = 0
    for b in range(HG.bit_length() - 1):
        bit = lax.rem(lax.div(group, 1 << b), 2)
        total = total + (1 << b) * ((1 - bit) if (k >> b) & 1 else bit)
    return total


def loop(low, high, body):
    if high - low <= 2:
        for i in range(low, high):
            body(i)
    else:

        def step(i, carry):
            body(i)
            return carry

        lax.fori_loop(low, high, step, 0)


def kernel(
    sizes, query, fresh, stale, caches, exps, attended, renewed,
    q_v, f_v, s_v, c_v, e_v, lim, dec, keys, values,
    qsend0, qsend1, qsend2, qgot0, qgot1, qgot2, osend0, osend1, osend2, ogot0, ogot1, ogot2,
    arrived0, arrived1, arrived2, in_sem, kv_send, kv_recv, fw_send, q_send, q_recv, o_send, o_recv,
):
    n, spread, rows, sub, unit, head, group_heads, stages = sizes
    cols = group_heads * head
    qsend, qgot = (qsend0, qsend1, qsend2), (qgot0, qgot1, qgot2)
    arrived = (arrived0, arrived1, arrived2)
    osend, ogot = (osend0, osend1, osend2), (ogot0, ogot1, ogot2)
    me = lax.axis_index("patch")
    group, member = lax.div(me, spread), lax.rem(me, spread)
    my_rows = pl.ds(pl.multiple_of(me * rows, 16), rows)

    loads = [
        pltpu.make_async_copy(a, b, in_sem.at[i])
        for i, (a, b) in enumerate(
            ((exps, e_v), (fresh, f_v), (stale, s_v), (query, q_v), (caches, c_v))
        )
    ]
    for load in loads[:4]:
        load.start()

    barrier = pltpu.get_barrier_semaphore()

    def greet(k):
        pl.semaphore_signal(
            barrier, inc=1, device_id={"patch": lax.rem(me + k, n)}, device_id_type=MESH
        )

    loop(1, n, greet)

    def remote(src, dst, send_sem, recv_sem, device):
        return pltpu.make_async_remote_copy(
            src_ref=src, dst_ref=dst, send_sem=send_sem, recv_sem=recv_sem,
            device_id={"patch": device}, device_id_type=MESH,
        )

    def landed(s, p):
        return arrived[s].at[p]

    def kv_copy(s, go):
        first, count = stages[s]
        return remote(
            dec.at[go, pl.ds(first, count)], landed(s, me),
            kv_send.at[s, go], kv_recv.at[s, me], go * spread + member,
        )

    def forward_copy(s, p, t):
        return remote(
            landed(s, p), landed(s, p),
            fw_send.at[s, lax.div(p, spread), t], kv_recv.at[s, p], group * spread + t,
        )

    def q_copy(s, d):
        return remote(qsend[s].at[d], qgot[s].at[me], q_send.at[s, d], q_recv.at[s, me], d)

    def o_copy(s, p):
        return remote(osend[s].at[p], ogot[s].at[me], o_send.at[s, p], o_recv.at[s, me], p)

    def spread_rows(x):
        if unit == sub:
            return x
        out = lax.broadcasted_iota(jnp.int32, (spread * unit, rows), 0)
        src = lax.broadcasted_iota(jnp.int32, (spread * unit, rows), 1)
        pick = (out // unit * sub + out % unit == src) & (out % unit < sub)
        return jnp.dot(
            pick.astype(jnp.bfloat16), x.astype(jnp.bfloat16), preferred_element_type=jnp.float32
        )

    def join_rows(x):
        if unit == sub:
            return x
        out = lax.broadcasted_iota(jnp.int32, (rows, spread * unit), 0)
        src = lax.broadcasted_iota(jnp.int32, (rows, spread * unit), 1)
        pick = out // sub * unit + out % sub == src
        return jnp.dot(
            pick.astype(jnp.bfloat16), x.astype(jnp.bfloat16), preferred_element_type=jnp.float32
        )

    loads[0].wait()
    head_count = e_v.shape[1]
    turn = lax.broadcasted_iota(jnp.int32, (head_count, head_count), 0)
    turn = (turn == lax.broadcasted_iota(jnp.int32, (head_count, head_count), 1)).astype(jnp.bfloat16)
    for which in (0, 1):
        power = (LIMIT * jnp.exp2(e_v[which].astype(jnp.float32))).astype(jnp.bfloat16)
        lim[which * rows : (which + 1) * rows] = lax.dot_general(
            power, turn, (((0,), (0,)), ((), ())), preferred_element_type=jnp.float32
        ).astype(jnp.bfloat16)
    for load in loads[1:4]:
        load.wait()

    def prepare(s, go):
        first, count = stages[s]
        width = count * head
        start = pl.multiple_of(go * cols + first * head, 128)
        window = pl.ds(start, width)
        which = lax.broadcasted_iota(jnp.int32, (head_count, width), 0)
        column = lax.broadcasted_iota(jnp.int32, (head_count, width), 1)
        one_hot = (which == go * group_heads + first + column // head).astype(jnp.bfloat16)
        limit = jnp.dot(lim[...], one_hot, preferred_element_type=jnp.float32)
        limit = limit.reshape(2, rows, width)
        old = s_v[:, :, window].astype(jnp.float32)
        residual = f_v[:, :, window].astype(jnp.float32) - old
        decoded = jnp.clip(residual, -limit, limit).astype(jnp.bfloat16)
        for j in range(count):
            dec[go, first + j] = decoded[:, :, j * head : (j + 1) * head]
        renewed[:, :, window] = (old + decoded.astype(jnp.float32)).astype(jnp.bfloat16)
        block = spread_rows(q_v[:, window].astype(jnp.float32))
        for t in range(spread):
            parts = [
                block[t * unit : (t + 1) * unit, j * head : (j + 1) * head] for j in range(count)
            ]
            spare = qsend[s].shape[1] - count * unit
            if spare:
                parts.append(jnp.zeros((spare, head), jnp.float32))
            qsend[s][go * spread + t] = jnp.concatenate(parts, axis=0).astype(jnp.bfloat16)

    for k in ORDER:
        prepare(0, partner_group(group, k))
    pl.semaphore_wait(barrier, n - 1)
    loads[4].start()

    for s in range(len(stages)):
        first, count = stages[s]
        for k in ORDER:
            go = partner_group(group, k)
            if s:
                prepare(s, go)
            if k:
                kv_copy(s, go).start()
                loop(0, spread, lambda t: q_copy(s, go * spread + t).start())
            else:
                arrived[s][me] = dec[group, pl.ds(first, count)]
                qgot[s][me] = qsend[s][me]

                def to_sibling(t):
                    @pl.when(t != member)
                    def _():
                        forward_copy(s, me, t).start()
                        q_copy(s, group * spread + t).start()

                loop(0, spread, to_sibling)

    loads[4].wait()

    def unpack(s):
        first, count = stages[s]

        def one_group(g):
            def arrive(t):
                @pl.when(g * spread + t != me)
                def _():
                    p = g * spread + t
                    remote(
                        osend[s].at[p], ogot[s].at[p], o_send.at[s, p], o_recv.at[s, p], p
                    ).wait_recv()

            loop(0, spread, arrive)
            got = ogot[s][pl.ds(g * spread, spread)].astype(jnp.float32)
            for j in range(count):
                piece = got[:, j * unit : (j + 1) * unit, :].reshape(spread * unit, head)
                start = pl.multiple_of(g * cols + (first + j) * head, 128)
                attended[:, pl.ds(start, head)] = join_rows(piece).astype(jnp.bfloat16)

        loop(0, HG, one_group)

    def give_back(s, p):
        @pl.when(p != me)
        def _():
            o_copy(s, p).start()

        @pl.when(p == me)
        def _():
            ogot[s][me] = osend[s][me]

    scale = head ** (-0.5) * math.log2(math.e)
    chunk = 8
    for s in range(len(stages)):
        first, count = stages[s]
        for k in ORDER[:-1]:
            p = partner_group(group, k) * spread + member
            forward_copy(s, p, 0).wait_recv()

            def pass_on(t):
                @pl.when(t != member)
                def _():
                    forward_copy(s, p, t).start()

            loop(0, spread, pass_on)

        def arrive_q(k):
            p = lax.rem(me + k, n)
            remote(qsend[s].at[p], qgot[s].at[p], q_send.at[s, p], q_recv.at[s, p], p).wait_recv()

        loop(1, n, arrive_q)

        def arrive_kv(t):
            @pl.when(t != member)
            def _():
                def one(g):
                    forward_copy(s, g * spread + t, 0).wait_recv()

                loop(0, HG, one)

        loop(0, spread, arrive_kv)

        for j in range(count):
            columns = pl.ds((first + j) * head, head)
            mine = pl.ds(pl.multiple_of(group * cols + (first + j) * head, 128), head)
            for which, store in ((0, keys), (1, values)):
                store[j] = (
                    c_v[0, which, :, columns].astype(jnp.float32)
                    + arrived[s][:, j, which].reshape(n * rows, head).astype(jnp.float32)
                ).astype(jnp.bfloat16)
                store[j, my_rows, :] = f_v[which, :, mine]

        for c0 in range(0, n, chunk):
            block = qgot[s][c0 : c0 + chunk].astype(jnp.float32)
            outs = []
            for j in range(count):
                q = block[:, j * unit : (j + 1) * unit, :].reshape(chunk * unit, head)
                scores = lax.dot_general(
                    q.astype(jnp.bfloat16), keys[j], (((1,), (1,)), ((), ())),
                    preferred_element_type=jnp.float32,
                )
                peak = jnp.max(scores, axis=-1, keepdims=True)
                raised = jnp.exp2((scores - peak) * scale)
                total = jnp.sum(raised, axis=-1, keepdims=True)
                mixed = jnp.dot(
                    raised.astype(jnp.bfloat16), values[j], preferred_element_type=jnp.float32
                )
                outs.append((mixed / total).reshape(chunk, unit, head))
            spare = osend[s].shape[1] - count * unit
            if spare:
                outs.append(jnp.zeros((chunk, spare, head), jnp.float32))
            osend[s][c0 : c0 + chunk] = jnp.concatenate(outs, axis=1).astype(jnp.bfloat16)

            loop(c0, c0 + chunk, lambda p: give_back(s, p))

    for s in range(len(stages)):
        unpack(s)

    for s in range(len(stages)):

        def left(k):
            p = lax.rem(me + k, n)
            q_copy(s, p).wait_send()
            o_copy(s, p).wait_send()

        loop(1, n, left)
        for k in ORDER[:-1]:
            kv_copy(s, partner_group(group, k)).wait_send()

        def left_sibling(t):
            @pl.when(t != member)
            def _():
                def one(g):
                    forward_copy(s, g * spread + member, t).wait_send()

                loop(0, HG, one)

        loop(0, spread, left_sibling)


def local(query, fresh_kv, own_stale, caches, exponents):
    rows, width = query.shape
    n = lax.axis_size("patch")
    spread = n // HG
    sub = rows // spread
    head = width // exponents.shape[2]
    group_heads = exponents.shape[2] // HG
    cols = width // HG
    unit = round_up(sub, 8)
    cuts = (0, 1, 3, group_heads)
    stages = tuple((a, b - a) for a, b in zip(cuts[:-1], cuts[1:]))
    tokens = caches.shape[2]
    most = max(count for _, count in stages)
    bf16 = jnp.bfloat16
    packs = [(n, round_up(count * unit, 16), head) for _, count in stages]
    dma = pltpu.SemaphoreType.DMA
    ns = len(stages)
    scratch = (
        [
            pltpu.VMEM(query.shape, bf16),
            pltpu.VMEM(fresh_kv.shape, bf16),
            pltpu.VMEM(own_stale.shape, bf16),
            pltpu.VMEM(caches.shape, bf16),
            pltpu.VMEM((2, exponents.shape[2], rows), jnp.int32),
            pltpu.VMEM((2 * rows, exponents.shape[2]), bf16),
            pltpu.VMEM((HG, group_heads, 2, rows, head), bf16),
            pltpu.VMEM((most, tokens, head), bf16),
            pltpu.VMEM((most, tokens, head), bf16),
        ]
        + [pltpu.VMEM(pack, bf16) for _ in range(4) for pack in packs]
        + [pltpu.VMEM((n, count, 2, rows, head), bf16) for _, count in stages]
        + [
            dma((5,)),
            dma((ns, HG)),
            dma((ns, n)),
            dma((ns, HG, spread)),
            dma((ns, n)),
            dma((ns, n)),
            dma((ns, n)),
            dma((ns, n)),
        ]
    )
    sizes = (n, spread, rows, sub, unit, head, group_heads, stages)
    anywhere = pl.BlockSpec(memory_space=pl.ANY)
    return pl.pallas_call(
        functools.partial(kernel, sizes),
        out_shape=(
            pltpu.VMEM(query.shape, bf16),
            pltpu.VMEM(fresh_kv.shape, bf16),
        ),
        in_specs=[pl.BlockSpec(memory_space=pltpu.HBM)] * 5,
        out_specs=(pl.BlockSpec(memory_space=pltpu.VMEM),) * 2,
        scratch_shapes=scratch,
        compiler_params=pltpu.CompilerParams(
            collective_id=0, has_side_effects=True, vmem_limit_bytes=60 * 1024 * 1024
        ),
    )(query, fresh_kv, own_stale, caches, exponents.transpose(0, 2, 1))


def solution(mesh):
    return jax.shard_map(
        local,
        mesh=mesh,
        in_specs=(
            P(("grp", "patch"), None),
            P(None, ("grp", "patch"), None),
            P(None, ("grp", "patch"), None),
            P(("grp", "patch"), None, None, None),
            P(None, ("grp", "patch"), None),
        ),
        out_specs=(P(("grp", "patch"), None), P(None, ("grp", "patch"), None)),
        check_vma=False,
    )
```
